32 devices in a mesh: dom: 16 (over z, y, core), repl: 2 (over x).
Axes of the slice: x: 2, y: 2, z: 4, core: 2. Of those that a mesh axis runs over, the one named last changes fastest.
Arguments:
- features: float32 [16384, 256], P(('dom', 'repl')), may hold values from -6 to 6
- weight: bfloat16 [256, 256], replicated, may hold values from -0.375 to 0.375
- bias_vector: float32 [256], replicated, may hold values from -0.5 to 0.5
- cotangent: bfloat16 [16384, 256], P(('dom', 'repl')), may hold values from -6 to 6
- near_tiles: bfloat16 [128, 128, 128], P(('dom', 'repl')), may hold values from -0.3125 to 0.3125
- near_offsets: int32 [32, 9], P(('dom', 'repl')), may hold values from 0 to 4, as said below
- near_cols: int32 [32, 4], P(('dom', 'repl')), may hold values from 0 to 3, as said below
- far_tiles: bfloat16 [32, 16, 1, 128, 128], P(('dom', 'repl')), may hold values from -0.3125 to 0.3125
- far_rows: int32 [32, 16, 1], P(('dom', 'repl')), may hold values from -1 to 7, as said below
- far_cols: int32 [32, 16, 1], P(('dom', 'repl')), may hold values from 0 to 3
Outputs:
- hidden: bfloat16 [16384, 256], P(('dom', 'repl'))
- grad_features: float32 [16384, 256], P(('dom', 'repl'))
- weight_grad: float32 [256, 256], replicated
The draws below stay inside these ranges and needn't reach their ends.
Inputs may be any that keep to these rules, and one draw needn't show every extreme that they name: `near_offsets`: each row is non-decreasing, begins with 0 and ends with 4. `near_cols`: within one tile row of one device the near tiles' columns differ and rise. `far_rows`: -1 marks an empty slot. A device's slots for the groups whose index of dom lies at most 1 step from its own around the cycle are never empty.
All inputs are finite; a program needn't handle non-finite values.
Results may differ from the reference program's by a relative error of at most 0.0075.
Values may be sent and summed in bfloat16 or wider, within the bound.
A program may use at most 128 MiB of HBM per device.

```python
import math
import jax
import jax.numpy as jnp
from jax import lax

FEAT = 256
BLOCK = 128
CAP = 1
RB_DEV = 4
RB_DOM = 8
NEAR = 4
SHARDS = 32
NODES = 16384
N_DOM = 16
N_REPL = 2


def near_pattern(key):
    base_key = jax.random.fold_in(key, 7)

    def one_shard(shard_index):
        shard_key = jax.random.fold_in(base_key, shard_index)
        picked = jnp.sort(jax.random.permutation(shard_key, RB_DOM * RB_DEV)[:NEAR].astype(jnp.int32))
        row_ids = picked // RB_DEV
        col_ids = picked % RB_DEV
        row_counts = jnp.sum((row_ids[None, :] == jnp.arange(RB_DOM, dtype=jnp.int32)[:, None]).astype(jnp.int32), axis=1)
        offsets = jnp.concatenate([jnp.zeros((1,), jnp.int32), jnp.cumsum(row_counts).astype(jnp.int32)])
        return (offsets, col_ids)
    return jax.vmap(one_shard)(jnp.arange(SHARDS, dtype=jnp.int32))


def draw_near_offsets(key, part):
    return near_pattern(key)[0]


def draw_near_cols(key, part):
    return near_pattern(key)[1]


def draw_far_rows(key, part):
    base_key = jax.random.fold_in(key, 11)
    keep_key = jax.random.fold_in(base_key, 1)
    row_key = jax.random.fold_in(base_key, 2)
    shard_ids = jnp.arange(SHARDS, dtype=jnp.int32)[:, None, None]
    group_ids = jnp.arange(N_DOM, dtype=jnp.int32)[None, :, None]
    own_group = shard_ids // N_REPL
    apart = jnp.abs(group_ids - own_group)
    cycle_gap = jnp.minimum(apart, N_DOM - apart)
    lucky = jax.random.randint(keep_key, (SHARDS, N_DOM, CAP), 0, 4, dtype=jnp.int32) == 0
    keep = jnp.logical_or(cycle_gap <= N_DOM // 16, lucky)
    rows = jax.random.randint(row_key, (SHARDS, N_DOM, CAP), 0, RB_DOM, dtype=jnp.int32)
    forced = jnp.logical_and(shard_ids == 0, group_ids == 0)
    rows = jnp.where(forced, RB_DOM - 1, rows)
    return jnp.where(keep, rows, -1).astype(jnp.int32)


def place_ends(entries, rng, least, top_value):
    longest = entries.shape.index(max(entries.shape))
    spots = []
    for shift in (0, 1):
        where = [jax.random.randint(jax.random.fold_in(rng, axis), (), 0, length) for axis, length in enumerate(entries.shape)]
        where[longest] = (where[longest] + shift) % entries.shape[longest]
        spots.append(tuple(where))
    return entries.at[spots[0]].set(least).at[spots[1]].set(top_value)


def steps_of(stream_key, dims, cuts, least, high):
    def one(position, shards_of):
        steps = jax.random.uniform(jax.random.fold_in(jax.random.fold_in(stream_key, 6), position), (shards_of,), jnp.float32, least / len(cuts), high / len(cuts))
        return jnp.repeat(jnp.exp(steps), dims[position] // shards_of).reshape((-1,) + (1,) * (len(dims) - position - 1))

    gain = one(*cuts[0])
    for cut in cuts[1:]:
        gain = gain * one(*cut)
    return gain


def centred(rng, shape, spread, limit, pieces=(), kind=jnp.bfloat16):
    array = spread * jax.random.normal(rng, shape, jnp.float32)
    if pieces:
        array = array * steps_of(rng, shape, pieces, -0.22, 0.18)
    return jnp.clip(array, -limit, limit).astype(kind)


def setup_inputs(seed: int = 0) -> dict:
    keys = jax.random.split(jax.random.key(seed), 11)
    return {
        "features": centred(keys[0], (NODES, FEAT), 1.0, 6.0, ((0, 32),), jnp.float32),
        "weight": centred(keys[1], (FEAT, FEAT), FEAT ** -0.5, 0.375),
        "bias_vector": jnp.clip(jax.random.uniform(keys[2], (FEAT,), jnp.float32, -0.5, 0.5), -0.5, 0.5),
        "cotangent": centred(keys[3], (NODES, FEAT), 1.0, 6.0, ((0, 32),)),
        "near_tiles": centred(keys[4], (SHARDS * NEAR, BLOCK, BLOCK), (BLOCK * (NEAR + N_DOM * CAP // 2) // RB_DEV) ** -0.5, 0.3125, ((0, 32),)),
        "near_offsets": draw_near_offsets(jax.random.fold_in(keys[10], 71), 0),
        "near_cols": draw_near_cols(jax.random.fold_in(keys[10], 71), 0),
        "far_tiles": centred(keys[7], (SHARDS, N_DOM, CAP, BLOCK, BLOCK), (BLOCK * (NEAR + N_DOM * CAP // 2) // RB_DEV) ** -0.5, 0.3125, ((0, 32),)),
        "far_rows": draw_far_rows(jax.random.fold_in(keys[10], 71), 0),
        "far_cols": place_ends(jax.random.randint(keys[9], (SHARDS, N_DOM, CAP), 0, RB_DEV), jax.random.fold_in(keys[9], 1), 0, RB_DEV - 1).astype(jnp.int32),
    }


def membership_flags(index, extent):
    return (index[..., None] == jnp.arange(extent, dtype=jnp.int32)).astype(jnp.float32)

def slot_rows(offsets):
    slots = jnp.arange(NEAR, dtype=jnp.int32)
    return lax.optimization_barrier(jnp.sum((offsets[1:, None] <= slots[None, :]).astype(jnp.int32), axis=0))

def matrix_result(form, left, right):
    return jnp.einsum(form, left, right, precision=lax.Precision.HIGHEST)

def activation_grad(pre_values, upstream):
    sigma = jax.nn.sigmoid(pre_values)
    return (upstream.astype(jnp.float32) * sigma * (1.0 + pre_values * (1.0 - sigma))).astype(jnp.bfloat16)

def reference(features, weight, bias_vector, cotangent, near_tiles, near_offsets, near_cols, far_tiles, far_rows, far_cols):
    reduced = features.astype(jnp.bfloat16)
    lanes = reduced.astype(jnp.float32).reshape(N_DOM, N_REPL, RB_DEV, BLOCK, FEAT)
    near_all = near_tiles.reshape(SHARDS, NEAR, BLOCK, BLOCK)

    def shard_parts(shard_index):
        dom_index = shard_index // N_REPL
        lane_index = shard_index % N_REPL
        nearby_square_tile = lax.dynamic_index_in_dim(near_all, shard_index, 0, keepdims=False).astype(jnp.float32)
        offsets = lax.dynamic_index_in_dim(near_offsets, shard_index, 0, keepdims=False)
        near_col = lax.dynamic_index_in_dim(near_cols, shard_index, 0, keepdims=False)
        far_tile = lax.dynamic_index_in_dim(far_tiles, shard_index, 0, keepdims=False).astype(jnp.float32)
        far_row = lax.dynamic_index_in_dim(far_rows, shard_index, 0, keepdims=False)
        far_col = lax.dynamic_index_in_dim(far_cols, shard_index, 0, keepdims=False)
        return (dom_index, lane_index, nearby_square_tile, membership_flags(slot_rows(offsets), RB_DOM), membership_flags(near_col, RB_DEV), far_tile, membership_flags(far_row, RB_DOM), membership_flags(far_col, RB_DEV))

    def forward_step(running, shard_index):
        dom_index, lane_index, nearby_square_tile, nearby_row_onehot, nearby_column_onehot, far_tile, far_row_hot, far_col_hot = shard_parts(shard_index)
        lane_blocks = lax.dynamic_index_in_dim(lanes, lane_index, 1, keepdims=False)
        local_block_list = lax.dynamic_index_in_dim(lane_blocks, dom_index, 0, keepdims=False)
        nearby_input_rows = matrix_result('el,lxh->exh', nearby_column_onehot, local_block_list)
        partial_sum = matrix_result('qr,qaf->raf', nearby_row_onehot, matrix_result('qab,qbf->qaf', nearby_square_tile, nearby_input_rows))
        far_inputs = matrix_result('kqc,kcbf->kqbf', far_col_hot, lane_blocks)
        partial_sum = partial_sum + matrix_result('kqr,kqaf->raf', far_row_hot, matrix_result('kqab,kqbf->kqaf', far_tile, far_inputs))
        current = lax.dynamic_index_in_dim(running, dom_index, 0, keepdims=False)
        running = lax.dynamic_update_index_in_dim(running, current + partial_sum, dom_index, 0)
        return (running, None)
    start_sum = jnp.zeros((N_DOM, RB_DOM, BLOCK, FEAT), jnp.float32)
    totals = lax.scan(forward_step, start_sum, jnp.arange(SHARDS, dtype=jnp.int32))[0]
    summed = totals.reshape(NODES, FEAT).astype(jnp.bfloat16)
    pre_act = jnp.dot(summed, weight, preferred_element_type=jnp.float32) + bias_vector
    hidden = jax.nn.silu(pre_act).astype(jnp.bfloat16)
    grad_pre = activation_grad(pre_act, cotangent)
    weight_grad = jnp.dot(summed.T, grad_pre, preferred_element_type=jnp.float32) * (1.0 / math.sqrt(NODES))
    grad_rows = jnp.dot(grad_pre, weight.T, preferred_element_type=jnp.float32).astype(jnp.bfloat16)
    grad_groups = grad_rows.astype(jnp.float32).reshape(N_DOM, RB_DOM, BLOCK, FEAT)

    def backward_step(running, shard_index):
        dom_index, lane_index, nearby_square_tile, nearby_row_onehot, nearby_column_onehot, far_tile, far_row_hot, far_col_hot = shard_parts(shard_index)
        cluster_block_list = lax.dynamic_index_in_dim(grad_groups, dom_index, 0, keepdims=False)
        nearby_output_rows = matrix_result('ml,mrx->lrx', nearby_column_onehot, matrix_result('ltp,ltk->lpk', nearby_square_tile, matrix_result('om,mgh->ogh', nearby_row_onehot, cluster_block_list)))
        far_out = matrix_result('kqc,kqbf->kcbf', far_col_hot, matrix_result('kqab,kqaf->kqbf', far_tile, matrix_result('kqr,rbf->kqbf', far_row_hot, cluster_block_list)))
        own_slot = lax.dynamic_index_in_dim(far_out, dom_index, 0, keepdims=False) + nearby_output_rows
        far_out = lax.dynamic_update_index_in_dim(far_out, own_slot, dom_index, 0)
        current = lax.dynamic_index_in_dim(running, lane_index, 1, keepdims=False)
        running = lax.dynamic_update_index_in_dim(running, current + far_out, lane_index, 1)
        return (running, None)
    grad_start = jnp.zeros((N_DOM, N_REPL, RB_DEV, BLOCK, FEAT), jnp.float32)
    grad_features = lax.scan(backward_step, grad_start, jnp.arange(SHARDS, dtype=jnp.int32))[0].reshape(NODES, FEAT)
    return (hidden, grad_features, weight_grad)
```

```python
import functools
import math

import jax
import jax.numpy as jnp
from jax import lax
from jax.experimental import pallas as pl
from jax.experimental.pallas import tpu as pltpu
from jax.sharding import PartitionSpec as P


def membership_flags(index, extent, dtype):
    return (index[..., None] == jnp.arange(extent, dtype=jnp.int32)).astype(dtype)


def slot_rows(offsets, slot_count):
    slots = jnp.arange(slot_count, dtype=jnp.int32)
    return jnp.sum((offsets[1:, None] <= slots[None, :]).astype(jnp.int32), axis=0)


def precise_total_sum(form, hot, values):
    return jnp.einsum(form, hot, values, precision=lax.Precision.HIGHEST)


def select(form, hot, values):
    return jnp.einsum(form, hot, values, preferred_element_type=jnp.float32).astype(jnp.bfloat16)


def tile_product(form, tiles, values):
    return jnp.einsum(form, tiles, values, preferred_element_type=jnp.float32)


def activation_grad(pre_values, upstream):
    sigma = jax.nn.sigmoid(pre_values)
    return (upstream.astype(jnp.float32) * sigma * (1.0 + pre_values * (1.0 - sigma))).astype(
        jnp.bfloat16
    )


def on_device(
    features,
    weight,
    bias_vector,
    cotangent,
    near_tiles,
    near_offsets,
    near_cols,
    far_tiles,
    far_rows,
    far_cols,
):
    rows_dev, feat_width = features.shape
    tile_size = near_tiles.shape[1]
    blocks_per_processor = rows_dev // tile_size
    dom_count = lax.axis_size("dom")
    repl_count = lax.axis_size("repl")
    blocks_dom = blocks_per_processor * repl_count
    near_count = near_tiles.shape[0]
    far_block = far_tiles[0]
    far_row_ids = far_rows[0]
    far_col_ids = far_cols[0]
    near_row_ids = slot_rows(near_offsets[0], near_count)
    nearby_column_index = near_cols[0]
    reduced = features.astype(jnp.bfloat16)
    local_block_list = reduced.reshape(blocks_per_processor, tile_size, feat_width)
    nearby_input_rows = select(
        "el,lxh->exh",
        membership_flags(nearby_column_index, blocks_per_processor, jnp.bfloat16),
        local_block_list,
    )
    near_prod = tile_product("qab,qbf->qaf", near_tiles, nearby_input_rows)
    partial_sum = precise_total_sum(
        "qr,qaf->raf", membership_flags(near_row_ids, blocks_dom, jnp.float32), near_prod
    )
    shard_rows = lax.all_gather(reduced, "dom", axis=0, tiled=True)
    range_count = shard_rows.shape[0] // rows_dev
    tiles = far_block
    row_ids = far_row_ids
    col_ids = far_col_ids
    source = shard_rows.reshape(range_count, blocks_per_processor, tile_size, feat_width)
    inputs = select(
        "kqc,kcbf->kqbf", membership_flags(col_ids, blocks_per_processor, jnp.bfloat16), source
    )
    far_prod = tile_product("kqab,kqbf->kqaf", tiles, inputs)
    partial_sum = partial_sum + precise_total_sum(
        "kqr,kqaf->raf", membership_flags(row_ids, blocks_dom, jnp.float32), far_prod
    )
    group_partial = partial_sum.reshape(blocks_dom * tile_size, feat_width)
    summed = lax.psum_scatter(group_partial, "repl", scatter_dimension=0, tiled=True).astype(
        jnp.bfloat16
    )
    pre_act = jnp.dot(summed, weight, preferred_element_type=jnp.float32) + bias_vector
    hidden = jax.nn.silu(pre_act).astype(jnp.bfloat16)
    grad_pre = activation_grad(pre_act, cotangent)
    weight_term = lax.dot_general(
        summed, grad_pre, (((0,), (0,)), ((), ())), preferred_element_type=jnp.float32
    )
    grad_rows = lax.dot_general(
        grad_pre, weight, (((1,), (1,)), ((), ())), preferred_element_type=jnp.float32
    ).astype(jnp.bfloat16)
    group_grad = lax.all_gather(grad_rows, "repl", axis=0, tiled=True)
    node_total = rows_dev * dom_count * repl_count
    weight_grad = lax.psum(weight_term, ("dom", "repl")) * (1.0 / math.sqrt(node_total))
    cluster_block_list = group_grad.reshape(blocks_dom, tile_size, feat_width)
    near_grads = select(
        "om,mgh->ogh", membership_flags(near_row_ids, blocks_dom, jnp.bfloat16), cluster_block_list
    )
    nearby_backward_pass = tile_product("ltp,ltk->lpk", near_tiles, near_grads)
    local_contribution = precise_total_sum(
        "ml,mrx->lrx",
        membership_flags(nearby_column_index, blocks_per_processor, jnp.float32),
        nearby_backward_pass,
    )
    row_count = rows_dev * lax.axis_size("dom")
    tiles = far_block
    row_ids = far_row_ids
    col_ids = far_col_ids
    far_grads = select(
        "kqr,rbf->kqbf", membership_flags(row_ids, blocks_dom, jnp.bfloat16), cluster_block_list
    )
    terms = tile_product("kqab,kqaf->kqbf", tiles, far_grads)
    placed = precise_total_sum(
        "kqc,kqbf->kcbf", membership_flags(col_ids, blocks_per_processor, jnp.float32), terms
    )
    far_grad = lax.psum_scatter(
        placed.reshape(row_count, feat_width).astype(jnp.bfloat16),
        "dom",
        scatter_dimension=0,
        tiled=True,
    ).astype(jnp.float32)
    grad_features = far_grad + local_contribution.reshape(rows_dev, feat_width)
    return (hidden, grad_features, weight_grad)


MESH = pl.DeviceIdType.MESH
FAST_PLANE = 4


def remote(src, dst, send_sem, recv_sem, dom, repl):
    return pltpu.make_async_remote_copy(
        src_ref=src,
        dst_ref=dst,
        send_sem=send_sem,
        recv_sem=recv_sem,
        device_id=(dom, repl),
        device_id_type=MESH,
    )


def layer_kernel(
    dom_count,
    near_count,
    scale,
    flags,
    features,
    weight,
    bias,
    cotangent,
    near_tiles,
    far_tiles,
    hidden,
    grad_features,
    weight_grad,
    own_feats,
    col_out,
    col_in,
    feat_out,
    feat_in,
    dense,
    far_flip,
    near_flip,
    part_out,
    part_in,
    part_own,
    summed,
    grad_pre,
    group_grad,
    term_out,
    term_in,
    share_out,
    share_in,
    plane_sum,
    final_share,
    col_send,
    col_recv,
    feat_send,
    feat_recv,
    part_send,
    part_recv,
    grad_send,
    grad_recv,
    term_send,
    term_recv,
    share_send,
    share_recv,
    plane_send,
    plane_recv,
    final_send,
    final_recv,
):
    f32, bf16 = jnp.float32, jnp.bfloat16
    dom, repl = lax.axis_index("dom"), lax.axis_index("repl")
    other = 1 - repl
    planes = dom_count // FAST_PLANE
    plane, lane = dom // FAST_PLANE, dom % FAST_PLANE
    rows_dev, feat = features.shape
    tile = near_tiles.shape[1]
    half = feat // 2
    blocks = rows_dev // tile
    rows_dom = 2 * blocks
    near_cols_at = near_count * rows_dom
    far_rows_at = near_cols_at + near_count * blocks
    far_cols_at = far_rows_at + dom_count * rows_dom

    def near_row(q, r):
        return flags[q * rows_dom + r]

    def near_col(q, c):
        return flags[near_cols_at + q * blocks + c]

    def far_row(k, r):
        return flags[far_rows_at + k * rows_dom + r]

    def far_col(k, c):
        return flags[far_cols_at + k * blocks + c]

    def at_distance(a, b):
        return ((plane + a) % planes) * FAST_PLANE + (lane + b) % FAST_PLANE

    steps = [(a, b) for a in (2, 3, 1, 0) for b in range(FAST_PLANE) if (a, b) != (0, 0)]
    steps = [(a, b) for a, b in steps if a < planes]
    mates = [(b, c) for b in range(FAST_PLANE) for c in range(2) if (b, c) != (0, 0)]

    def mate(b, c):
        return plane * FAST_PLANE + (lane + b) % FAST_PLANE, (repl + c) % 2

    barrier = pltpu.get_barrier_semaphore()
    for a, b in steps:
        pl.semaphore_signal(barrier, inc=1, device_id=(at_distance(a, b), repl), device_id_type=MESH)
    for b in range(FAST_PLANE):
        pl.semaphore_signal(barrier, inc=1, device_id=mate(b, 1), device_id_type=MESH)
    col_out[...] = jnp.zeros_like(col_out)
    for k in range(dom_count):
        for c in range(blocks):
            col_out[k, c : c + 1] = jnp.full((1, half), far_col(k, c), f32)
    col_in[dom] = col_out[dom]
    for h in range(2):
        own_feats[h] = features[:, h * half : (h + 1) * half].astype(bf16)
    pl.semaphore_wait(barrier, len(steps) + FAST_PLANE)

    def col_copy(i, peer):
        return remote(
            col_out.at[peer], col_in.at[dom], col_send.at[i], col_recv.at[i], peer, repl
        )

    def source(i):
        a, b = steps[i]
        return at_distance((planes - a) % planes, (FAST_PLANE - b) % FAST_PLANE)

    for i, (a, b) in enumerate(steps):
        col_copy(i, at_distance(a, b)).start()

    def chosen(k, h):
        want = col_in[k]
        pick = jnp.zeros((tile, half), f32)
        for c in range(blocks):
            block = features[c * tile : (c + 1) * tile, h * half : (h + 1) * half]
            pick = pick + block * want[c : c + 1]
        return pick.astype(bf16)

    def feat_copy(h, i, peer):
        return remote(
            feat_out.at[h, i],
            feat_in.at[h, pl.ds(pl.multiple_of(dom * tile, tile), tile)],
            feat_send.at[h, i],
            feat_recv.at[h, i],
            peer,
            repl,
        )

    opposite = {}
    for i, (a, b) in enumerate(steps):
        opposite[i] = steps.index(((planes - a) % planes, (FAST_PLANE - b) % FAST_PLANE))
    for h in range(2):
        for i, (a, b) in enumerate(steps):
            peer = at_distance(a, b)
            if h == 0:
                col_copy(opposite[i], peer).wait_recv()
            feat_out[h, i] = chosen(peer, h)
            feat_copy(h, i, peer).start()
    for h in range(2):
        feat_in[h, pl.ds(pl.multiple_of(dom * tile, tile), tile)] = chosen(dom, h)

    for q in range(near_count):
        near_flip[q] = near_tiles[q].astype(f32).T.astype(bf16)
    for r in range(rows_dom):
        for c in range(blocks):
            block = jnp.zeros((tile, tile), f32)
            for q in range(near_count):
                block = block + near_tiles[q].astype(f32) * (near_row(q, r) * near_col(q, c))
            dense[r * tile : (r + 1) * tile, c * tile : (c + 1) * tile] = block.astype(bf16)

    def build(k, carry):
        block = far_tiles[k].astype(f32)
        far_flip[k] = block.T.astype(bf16)
        at = pl.ds(pl.multiple_of(rows_dev + k * tile, tile), tile)
        for r in range(rows_dom):
            dense[r * tile : (r + 1) * tile, at] = (block * far_row(k, r)).astype(bf16)
        return carry

    lax.fori_loop(0, dom_count, build, 0)

    def aggregate(owner, h):
        at = pl.ds(pl.multiple_of(owner * rows_dev, rows_dev), rows_dev)
        return jnp.dot(dense[at, :rows_dev], own_feats[h], preferred_element_type=f32) + jnp.dot(
            dense[at, rows_dev:], feat_in[h], preferred_element_type=f32
        )

    def part_copy(h):
        return remote(
            part_out.at[h], part_in.at[h], part_send.at[h], part_recv.at[h], dom, other
        )

    for h in range(2):
        for i, (a, b) in enumerate(steps):
            feat_copy(h, i, at_distance(a, b)).wait_recv()
        part_out[h] = aggregate(other, h).astype(bf16)
        part_copy(h).start()
        part_own[h] = aggregate(repl, h)
    for h in range(2):
        part_copy(h).wait_recv()
        summed[:, h * half : (h + 1) * half] = (part_own[h] + part_in[h].astype(f32)).astype(bf16)

    pre_act = jnp.dot(summed[...], weight[...], preferred_element_type=f32) + bias[...]
    sigma = 1.0 / (1.0 + jnp.exp(-pre_act))
    hidden[...] = (pre_act * sigma).astype(bf16)
    grad_pre[...] = (
        cotangent[...].astype(f32) * sigma * (1.0 + pre_act * (1.0 - sigma))
    ).astype(bf16)

    mine = pl.ds(pl.multiple_of(repl * rows_dev, rows_dev), rows_dev)

    def grad_copy(h):
        return remote(
            group_grad.at[h, mine],
            group_grad.at[h, mine],
            grad_send.at[h],
            grad_recv.at[h],
            dom,
            other,
        )

    for h in range(2):
        group_grad[h, mine] = lax.dot_general(
            grad_pre[...],
            weight[h * half : (h + 1) * half, :],
            (((1,), (1,)), ((), ())),
            preferred_element_type=f32,
        ).astype(bf16)
        grad_copy(h).start()

    place = lane * 2 + repl
    shares = 2 * FAST_PLANE
    share_rows = feat // shares
    for p in range(shares):
        share_out[p] = lax.dot_general(
            summed[:, p * share_rows : (p + 1) * share_rows],
            grad_pre[...],
            (((0,), (0,)), ((), ())),
            preferred_element_type=f32,
        ).astype(bf16)
    share_in[place] = share_out[place]

    def share_copy(i):
        to_dom, to_repl = mate(*mates[i])
        return remote(
            share_out.at[(to_dom % FAST_PLANE) * 2 + to_repl],
            share_in.at[place],
            share_send.at[i],
            share_recv.at[i],
            to_dom,
            to_repl,
        )

    for i in range(len(mates)):
        share_copy(i).start()

    def far_term(k, h):
        rows = jnp.zeros((tile, half), f32)
        for r in range(rows_dom):
            rows = rows + group_grad[h, r * tile : (r + 1) * tile].astype(f32) * far_row(k, r)
        return jnp.dot(far_flip[k], rows.astype(bf16), preferred_element_type=f32)

    def term_copy(h, i, peer):
        return remote(
            term_out.at[h, i], term_in.at[h, dom], term_send.at[h, i], term_recv.at[h, i], peer, repl
        )

    for h in range(2):
        grad_copy(h).wait_recv()
        for i, (a, b) in enumerate(steps):
            peer = at_distance(a, b)
            term_out[h, i] = far_term(peer, h).astype(bf16)
            term_copy(h, i, peer).start()
        term_in[h, dom] = far_term(dom, h).astype(bf16)

    for i in range(len(mates)):
        share_copy(i).wait_recv()
    total = share_in[0].astype(f32)
    for p in range(1, shares):
        total = total + share_in[p].astype(f32)
    plane_sum[plane] = total.astype(bf16)

    def plane_copy(a):
        return remote(
            plane_sum.at[plane],
            plane_sum.at[plane],
            plane_send.at[a - 1],
            plane_recv.at[a - 1],
            at_distance(a, 0),
            repl,
        )

    for a in range(1, planes):
        plane_copy(a).start()

    for h in range(2):
        at = slice(h * half, (h + 1) * half)
        near_terms = []
        for q in range(near_count):
            rows = jnp.zeros((tile, half), f32)
            for r in range(rows_dom):
                rows = rows + group_grad[h, r * tile : (r + 1) * tile].astype(f32) * near_row(q, r)
            near_terms.append(jnp.dot(near_flip[q], rows.astype(bf16), preferred_element_type=f32))
        for c in range(blocks):
            block = jnp.zeros((tile, half), f32)
            for q in range(near_count):
                block = block + near_terms[q] * near_col(q, c)
            grad_features[c * tile : (c + 1) * tile, at] = block

    for a in range(1, planes):
        plane_copy(a).wait_recv()
    total = plane_sum[0].astype(f32)
    for z in range(1, planes):
        total = total + plane_sum[z].astype(f32)
    final_share[place] = total * scale

    def final_copy(i):
        to_dom, to_repl = mate(*mates[i])
        return remote(
            final_share.at[place],
            final_share.at[place],
            final_send.at[i],
            final_recv.at[i],
            to_dom,
            to_repl,
        )

    for i in range(len(mates)):
        final_copy(i).start()

    def place_term(k, h):
        at = slice(h * half, (h + 1) * half)
        want = col_in[k]
        term = term_in[h, k].astype(f32)
        for c in range(blocks):
            rows = slice(c * tile, (c + 1) * tile)
            grad_features[rows, at] += term * want[c : c + 1]

    for h in range(2):
        place_term(dom, h)
        for i in range(len(steps)):
            term_copy(h, i, at_distance(*steps[i])).wait_recv()
            place_term(source(i), h)

    for i in range(len(mates)):
        final_copy(i).wait_recv()
    for p in range(shares):
        weight_grad[p * share_rows : (p + 1) * share_rows, :] = final_share[p]

    for i, (a, b) in enumerate(steps):
        peer = at_distance(a, b)
        col_copy(i, peer).wait_send()
        for h in range(2):
            feat_copy(h, i, peer).wait_send()
            term_copy(h, i, peer).wait_send()
    for h in range(2):
        part_copy(h).wait_send()
        grad_copy(h).wait_send()
    for i in range(len(mates)):
        share_copy(i).wait_send()
        final_copy(i).wait_send()
    for a in range(1, planes):
        plane_copy(a).wait_send()


def fused_on_device(
    features,
    weight,
    bias_vector,
    cotangent,
    near_tiles,
    near_offsets,
    near_cols,
    far_tiles,
    far_rows,
    far_cols,
):
    rows_dev, feat = features.shape
    tile = near_tiles.shape[1]
    near_count = near_tiles.shape[0]
    dom_count = lax.axis_size("dom")
    half = feat // 2
    peers = dom_count - 1
    shares = 2 * FAST_PLANE
    mates = shares - 1
    planes = dom_count // FAST_PLANE
    blocks = rows_dev // tile
    near_rows = slot_rows(near_offsets[0], near_count)
    hot = (
        membership_flags(near_rows, 2 * blocks, jnp.float32),
        membership_flags(near_cols[0], blocks, jnp.float32),
        membership_flags(far_rows.reshape(-1), 2 * blocks, jnp.float32),
        membership_flags(far_cols.reshape(-1), blocks, jnp.float32),
    )
    flags = jnp.concatenate([part.reshape(-1) for part in hot])
    scale = 1.0 / math.sqrt(rows_dev * dom_count * 2)
    bf16, f32 = jnp.bfloat16, jnp.float32
    vmem = pl.BlockSpec(memory_space=pltpu.VMEM)
    dma = pltpu.SemaphoreType.DMA
    return pl.pallas_call(
        functools.partial(layer_kernel, dom_count, near_count, scale),
        out_shape=(
            jax.ShapeDtypeStruct((rows_dev, feat), bf16),
            jax.ShapeDtypeStruct((rows_dev, feat), f32),
            jax.ShapeDtypeStruct((feat, feat), f32),
        ),
        in_specs=[pl.BlockSpec(memory_space=pltpu.SMEM)] + [vmem] * 6,
        out_specs=(vmem, vmem, vmem),
        scratch_shapes=[
            pltpu.VMEM((2, rows_dev, half), bf16),
            pltpu.VMEM((dom_count, 8, half), f32),
            pltpu.VMEM((dom_count, 8, half), f32),
            pltpu.VMEM((2, peers, tile, half), bf16),
            pltpu.VMEM((2, dom_count * tile, half), bf16),
            pltpu.VMEM((2 * rows_dev, rows_dev + dom_count * tile), bf16),
            pltpu.VMEM((dom_count, tile, tile), bf16),
            pltpu.VMEM((near_count, tile, tile), bf16),
            pltpu.VMEM((2, rows_dev, half), bf16),
            pltpu.VMEM((2, rows_dev, half), bf16),
            pltpu.VMEM((2, rows_dev, half), f32),
            pltpu.VMEM((rows_dev, feat), bf16),
            pltpu.VMEM((rows_dev, feat), bf16),
            pltpu.VMEM((2, 2 * rows_dev, half), bf16),
            pltpu.VMEM((2, peers, tile, half), bf16),
            pltpu.VMEM((2, dom_count, tile, half), bf16),
            pltpu.VMEM((shares, feat // shares, feat), bf16),
            pltpu.VMEM((shares, feat // shares, feat), bf16),
            pltpu.VMEM((planes, feat // shares, feat), bf16),
            pltpu.VMEM((shares, feat // shares, feat), f32),
            dma((peers,)),
            dma((peers,)),
            dma((2, peers)),
            dma((2, peers)),
            dma((2,)),
            dma((2,)),
            dma((2,)),
            dma((2,)),
            dma((2, peers)),
            dma((2, peers)),
            dma((mates,)),
            dma((mates,)),
            dma((planes - 1,)),
            dma((planes - 1,)),
            dma((mates,)),
            dma((mates,)),
        ],
        compiler_params=pltpu.CompilerParams(
            collective_id=0, has_side_effects=True, vmem_limit_bytes=40 * 1024 * 1024
        ),
    )(
        flags,
        features,
        weight,
        bias_vector.reshape(1, feat),
        cotangent,
        near_tiles,
        far_tiles.reshape(dom_count, tile, tile),
    )


def fits_one_kernel(mesh):
    return mesh.shape["repl"] == 2 and mesh.shape["dom"] == 4 * FAST_PLANE


def solution(mesh):
    placed = (
        P(("dom", "repl"), None),
        P(),
        P(),
        P(("dom", "repl"), None),
        P(("dom", "repl"), None, None),
        P(("dom", "repl"), None),
        P(("dom", "repl"), None),
        P(("dom", "repl"), None, None, None, None),
        P(("dom", "repl"), None, None),
        P(("dom", "repl"), None, None),
    )
    return jax.shard_map(
        fused_on_device if fits_one_kernel(mesh) else on_device,
        mesh=mesh,
        in_specs=placed,
        out_specs=(P(("dom", "repl"), None), P(("dom", "repl"), None), P()),
        check_vma=False,
    )
```

```python
import functools
import math

import jax
import jax.numpy as jnp
from jax import lax
from jax.experimental import pallas as pl
from jax.experimental.pallas import tpu as pltpu
from jax.sharding import PartitionSpec as P


def membership_flags(index, extent, dtype):
    return (index[..., None] == jnp.arange(extent, dtype=jnp.int32)).astype(dtype)


def slot_rows(offsets, slot_count):
    slots = jnp.arange(slot_count, dtype=jnp.int32)
    return jnp.sum((offsets[1:, None] <= slots[None, :]).astype(jnp.int32), axis=0)


def precise_total_sum(form, hot, values):
    return jnp.einsum(form, hot, values, precision=lax.Precision.HIGHEST)


def select(form, hot, values):
    return jnp.einsum(form, hot, values, preferred_element_type=jnp.float32).astype(jnp.bfloat16)


def tile_product(form, tiles, values):
    return jnp.einsum(form, tiles, values, preferred_element_type=jnp.float32)


def activation_grad(pre_values, upstream):
    sigma = jax.nn.sigmoid(pre_values)
    return (upstream.astype(jnp.float32) * sigma * (1.0 + pre_values * (1.0 - sigma))).astype(
        jnp.bfloat16
    )


def on_device(
    features,
    weight,
    bias_vector,
    cotangent,
    near_tiles,
    near_offsets,
    near_cols,
    far_tiles,
    far_rows,
    far_cols,
):
    rows_dev, feat_width = features.shape
    tile_size = near_tiles.shape[1]
    blocks_per_processor = rows_dev // tile_size
    dom_count = lax.axis_size("dom")
    repl_count = lax.axis_size("repl")
    blocks_dom = blocks_per_processor * repl_count
    near_count = near_tiles.shape[0]
    far_block = far_tiles[0]
    far_row_ids = far_rows[0]
    far_col_ids = far_cols[0]
    near_row_ids = slot_rows(near_offsets[0], near_count)
    nearby_column_index = near_cols[0]
    reduced = features.astype(jnp.bfloat16)
    local_block_list = reduced.reshape(blocks_per_processor, tile_size, feat_width)
    nearby_input_rows = select(
        "el,lxh->exh",
        membership_flags(nearby_column_index, blocks_per_processor, jnp.bfloat16),
        local_block_list,
    )
    near_prod = tile_product("qab,qbf->qaf", near_tiles, nearby_input_rows)
    partial_sum = precise_total_sum(
        "qr,qaf->raf", membership_flags(near_row_ids, blocks_dom, jnp.float32), near_prod
    )
    shard_rows = lax.all_gather(reduced, "dom", axis=0, tiled=True)
    range_count = shard_rows.shape[0] // rows_dev
    tiles = far_block
    row_ids = far_row_ids
    col_ids = far_col_ids
    source = shard_rows.reshape(range_count, blocks_per_processor, tile_size, feat_width)
    inputs = select(
        "kqc,kcbf->kqbf", membership_flags(col_ids, blocks_per_processor, jnp.bfloat16), source
    )
    far_prod = tile_product("kqab,kqbf->kqaf", tiles, inputs)
    partial_sum = partial_sum + precise_total_sum(
        "kqr,kqaf->raf", membership_flags(row_ids, blocks_dom, jnp.float32), far_prod
    )
    group_partial = partial_sum.reshape(blocks_dom * tile_size, feat_width)
    summed = lax.psum_scatter(group_partial, "repl", scatter_dimension=0, tiled=True).astype(
        jnp.bfloat16
    )
    pre_act = jnp.dot(summed, weight, preferred_element_type=jnp.float32) + bias_vector
    hidden = jax.nn.silu(pre_act).astype(jnp.bfloat16)
    grad_pre = activation_grad(pre_act, cotangent)
    weight_term = lax.dot_general(
        summed, grad_pre, (((0,), (0,)), ((), ())), preferred_element_type=jnp.float32
    )
    grad_rows = lax.dot_general(
        grad_pre, weight, (((1,), (1,)), ((), ())), preferred_element_type=jnp.float32
    ).astype(jnp.bfloat16)
    group_grad = lax.all_gather(grad_rows, "repl", axis=0, tiled=True)
    node_total = rows_dev * dom_count * repl_count
    weight_grad = lax.psum(weight_term, ("dom", "repl")) * (1.0 / math.sqrt(node_total))
    cluster_block_list = group_grad.reshape(blocks_dom, tile_size, feat_width)
    near_grads = select(
        "om,mgh->ogh", membership_flags(near_row_ids, blocks_dom, jnp.bfloat16), cluster_block_list
    )
    nearby_backward_pass = tile_product("ltp,ltk->lpk", near_tiles, near_grads)
    local_contribution = precise_total_sum(
        "ml,mrx->lrx",
        membership_flags(nearby_column_index, blocks_per_processor, jnp.float32),
        nearby_backward_pass,
    )
    row_count = rows_dev * lax.axis_size("dom")
    tiles = far_block
    row_ids = far_row_ids
    col_ids = far_col_ids
    far_grads = select(
        "kqr,rbf->kqbf", membership_flags(row_ids, blocks_dom, jnp.bfloat16), cluster_block_list
    )
    terms = tile_product("kqab,kqaf->kqbf", tiles, far_grads)
    placed = precise_total_sum(
        "kqc,kqbf->kcbf", membership_flags(col_ids, blocks_per_processor, jnp.float32), terms
    )
    far_grad = lax.psum_scatter(
        placed.reshape(row_count, feat_width).astype(jnp.bfloat16),
        "dom",
        scatter_dimension=0,
        tiled=True,
    ).astype(jnp.float32)
    grad_features = far_grad + local_contribution.reshape(rows_dev, feat_width)
    return (hidden, grad_features, weight_grad)


MESH = pl.DeviceIdType.MESH
FAST_PLANE = 4


def remote(src, dst, send_sem, recv_sem, dom, repl):
    return pltpu.make_async_remote_copy(
        src_ref=src,
        dst_ref=dst,
        send_sem=send_sem,
        recv_sem=recv_sem,
        device_id=(dom, repl),
        device_id_type=MESH,
    )


def layer_kernel(
    dom_count,
    near_count,
    scale,
    flags,
    features_hbm,
    weight_hbm,
    bias,
    cotangent_hbm,
    near_hbm,
    far_hbm,
    hidden,
    grad_features,
    weight_grad,
    features,
    weight,
    cotangent,
    near_tiles,
    far_tiles,
    load_sem,
    own_feats,
    col_out,
    col_in,
    feat_out,
    feat_in,
    dense,
    far_flip,
    near_flip,
    part_out,
    part_in,
    part_own,
    summed,
    grad_pre,
    group_grad,
    term_out,
    term_in,
    share_out,
    share_in,
    plane_sum,
    final_share,
    col_send,
    col_recv,
    feat_send,
    feat_recv,
    part_send,
    part_recv,
    grad_send,
    grad_recv,
    term_send,
    term_recv,
    share_send,
    share_recv,
    plane_send,
    plane_recv,
    final_send,
    final_recv,
):
    pairs = (
        (features_hbm, features),
        (near_hbm, near_tiles),
        (far_hbm, far_tiles),
        (weight_hbm, weight),
        (cotangent_hbm, cotangent),
    )
    loads = [pltpu.make_async_copy(a, b, load_sem.at[i]) for i, (a, b) in enumerate(pairs)]
    for load in loads:
        load.start()
    f32, bf16 = jnp.float32, jnp.bfloat16
    dom, repl = lax.axis_index("dom"), lax.axis_index("repl")
    other = 1 - repl
    planes = dom_count // FAST_PLANE
    plane, lane = dom // FAST_PLANE, dom % FAST_PLANE
    rows_dev, feat = features.shape
    tile = near_tiles.shape[1]
    half = feat // 2
    blocks = rows_dev // tile
    rows_dom = 2 * blocks
    near_cols_at = near_count * rows_dom
    far_rows_at = near_cols_at + near_count * blocks
    far_cols_at = far_rows_at + dom_count * rows_dom

    def near_row(q, r):
        return flags[q * rows_dom + r]

    def near_col(q, c):
        return flags[near_cols_at + q * blocks + c]

    def far_row(k, r):
        return flags[far_rows_at + k * rows_dom + r]

    def far_col(k, c):
        return flags[far_cols_at + k * blocks + c]

    def at_distance(a, b):
        return ((plane + a) % planes) * FAST_PLANE + (lane + b) % FAST_PLANE

    steps = [(a, b) for a in (2, 3, 1, 0) for b in range(FAST_PLANE) if (a, b) != (0, 0)]
    steps = [(a, b) for a, b in steps if a < planes]
    mates = [(b, c) for b in range(FAST_PLANE) for c in range(2) if (b, c) != (0, 0)]

    def mate(b, c):
        return plane * FAST_PLANE + (lane + b) % FAST_PLANE, (repl + c) % 2

    barrier = pltpu.get_barrier_semaphore()
    for a, b in steps:
        pl.semaphore_signal(barrier, inc=1, device_id=(at_distance(a, b), repl), device_id_type=MESH)
    for b in range(FAST_PLANE):
        pl.semaphore_signal(barrier, inc=1, device_id=mate(b, 1), device_id_type=MESH)
    col_out[...] = jnp.zeros_like(col_out)
    for k in range(dom_count):
        for c in range(blocks):
            col_out[k, c : c + 1] = jnp.full((1, half), far_col(k, c), f32)
    col_in[dom] = col_out[dom]
    loads[0].wait()
    for h in range(2):
        own_feats[h] = features[:, h * half : (h + 1) * half].astype(bf16)
    pl.semaphore_wait(barrier, len(steps) + FAST_PLANE)

    def col_copy(i, peer):
        return remote(
            col_out.at[peer], col_in.at[dom], col_send.at[i], col_recv.at[i], peer, repl
        )

    def source(i):
        a, b = steps[i]
        return at_distance((planes - a) % planes, (FAST_PLANE - b) % FAST_PLANE)

    for i, (a, b) in enumerate(steps):
        col_copy(i, at_distance(a, b)).start()

    def chosen(k, h):
        want = col_in[k]
        pick = jnp.zeros((tile, half), f32)
        for c in range(blocks):
            block = features[c * tile : (c + 1) * tile, h * half : (h + 1) * half]
            pick = pick + block * want[c : c + 1]
        return pick.astype(bf16)

    def feat_copy(h, i, peer):
        return remote(
            feat_out.at[h, i],
            feat_in.at[h, pl.ds(pl.multiple_of(dom * tile, tile), tile)],
            feat_send.at[h, i],
            feat_recv.at[h, i],
            peer,
            repl,
        )

    opposite = {}
    for i, (a, b) in enumerate(steps):
        opposite[i] = steps.index(((planes - a) % planes, (FAST_PLANE - b) % FAST_PLANE))
    for h in range(2):
        for i, (a, b) in enumerate(steps):
            peer = at_distance(a, b)
            if h == 0:
                col_copy(opposite[i], peer).wait_recv()
            feat_out[h, i] = chosen(peer, h)
            feat_copy(h, i, peer).start()
    for h in range(2):
        feat_in[h, pl.ds(pl.multiple_of(dom * tile, tile), tile)] = chosen(dom, h)

    loads[1].wait()
    loads[2].wait()
    for q in range(near_count):
        near_flip[q] = near_tiles[q].astype(f32).T.astype(bf16)
    for r in range(rows_dom):
        for c in range(blocks):
            block = jnp.zeros((tile, tile), f32)
            for q in range(near_count):
                block = block + near_tiles[q].astype(f32) * (near_row(q, r) * near_col(q, c))
            dense[r * tile : (r + 1) * tile, c * tile : (c + 1) * tile] = block.astype(bf16)

    def build(k, carry):
        block = far_tiles[k].astype(f32)
        far_flip[k] = block.T.astype(bf16)
        at = pl.ds(pl.multiple_of(rows_dev + k * tile, tile), tile)
        for r in range(rows_dom):
            dense[r * tile : (r + 1) * tile, at] = (block * far_row(k, r)).astype(bf16)
        return carry

    lax.fori_loop(0, dom_count, build, 0)

    def aggregate(owner, h):
        at = pl.ds(pl.multiple_of(owner * rows_dev, rows_dev), rows_dev)
        return jnp.dot(dense[at, :rows_dev], own_feats[h], preferred_element_type=f32) + jnp.dot(
            dense[at, rows_dev:], feat_in[h], preferred_element_type=f32
        )

    def part_copy(h):
        return remote(
            part_out.at[h], part_in.at[h], part_send.at[h], part_recv.at[h], dom, other
        )

    for h in range(2):
        for i, (a, b) in enumerate(steps):
            feat_copy(h, i, at_distance(a, b)).wait_recv()
        part_out[h] = aggregate(other, h).astype(bf16)
        part_copy(h).start()
        part_own[h] = aggregate(repl, h)
    for h in range(2):
        part_copy(h).wait_recv()
        summed[:, h * half : (h + 1) * half] = (part_own[h] + part_in[h].astype(f32)).astype(bf16)

    loads[3].wait()
    loads[4].wait()
    pre_act = jnp.dot(summed[...], weight[...], preferred_element_type=f32) + bias[...]
    sigma = 1.0 / (1.0 + jnp.exp(-pre_act))
    hidden[...] = (pre_act * sigma).astype(bf16)
    grad_pre[...] = (
        cotangent[...].astype(f32) * sigma * (1.0 + pre_act * (1.0 - sigma))
    ).astype(bf16)

    mine = pl.ds(pl.multiple_of(repl * rows_dev, rows_dev), rows_dev)

    def grad_copy(h):
        return remote(
            group_grad.at[h, mine],
            group_grad.at[h, mine],
            grad_send.at[h],
            grad_recv.at[h],
            dom,
            other,
        )

    for h in range(2):
        group_grad[h, mine] = lax.dot_general(
            grad_pre[...],
            weight[h * half : (h + 1) * half, :],
            (((1,), (1,)), ((), ())),
            preferred_element_type=f32,
        ).astype(bf16)
        grad_copy(h).start()

    place = lane * 2 + repl
    shares = 2 * FAST_PLANE
    share_rows = feat // shares
    for p in range(shares):
        share_out[p] = lax.dot_general(
            summed[:, p * share_rows : (p + 1) * share_rows],
            grad_pre[...],
            (((0,), (0,)), ((), ())),
            preferred_element_type=f32,
        ).astype(bf16)
    share_in[place] = share_out[place]

    def share_copy(i):
        to_dom, to_repl = mate(*mates[i])
        return remote(
            share_out.at[(to_dom % FAST_PLANE) * 2 + to_repl],
            share_in.at[place],
            share_send.at[i],
            share_recv.at[i],
            to_dom,
            to_repl,
        )

    for i in range(len(mates)):
        share_copy(i).start()

    def far_term(k, h):
        rows = jnp.zeros((tile, half), f32)
        for r in range(rows_dom):
            rows = rows + group_grad[h, r * tile : (r + 1) * tile].astype(f32) * far_row(k, r)
        return jnp.dot(far_flip[k], rows.astype(bf16), preferred_element_type=f32)

    def term_copy(h, i, peer):
        return remote(
            term_out.at[h, i], term_in.at[h, dom], term_send.at[h, i], term_recv.at[h, i], peer, repl
        )

    for h in range(2):
        grad_copy(h).wait_recv()
        for i, (a, b) in enumerate(steps):
            peer = at_distance(a, b)
            term_out[h, i] = far_term(peer, h).astype(bf16)
            term_copy(h, i, peer).start()
        term_in[h, dom] = far_term(dom, h).astype(bf16)

    for i in range(len(mates)):
        share_copy(i).wait_recv()
    total = share_in[0].astype(f32)
    for p in range(1, shares):
        total = total + share_in[p].astype(f32)
    plane_sum[plane] = total.astype(bf16)

    def plane_copy(a):
        return remote(
            plane_sum.at[plane],
            plane_sum.at[plane],
            plane_send.at[a - 1],
            plane_recv.at[a - 1],
            at_distance(a, 0),
            repl,
        )

    for a in range(1, planes):
        plane_copy(a).start()

    for h in range(2):
        at = slice(h * half, (h + 1) * half)
        near_terms = []
        for q in range(near_count):
            rows = jnp.zeros((tile, half), f32)
            for r in range(rows_dom):
                rows = rows + group_grad[h, r * tile : (r + 1) * tile].astype(f32) * near_row(q, r)
            near_terms.append(jnp.dot(near_flip[q], rows.astype(bf16), preferred_element_type=f32))
        for c in range(blocks):
            block = jnp.zeros((tile, half), f32)
            for q in range(near_count):
                block = block + near_terms[q] * near_col(q, c)
            grad_features[c * tile : (c + 1) * tile, at] = block

    for a in range(1, planes):
        plane_copy(a).wait_recv()
    total = plane_sum[0].astype(f32)
    for z in range(1, planes):
        total = total + plane_sum[z].astype(f32)
    final_share[place] = total * scale

    def final_copy(i):
        to_dom, to_repl = mate(*mates[i])
        return remote(
            final_share.at[place],
            final_share.at[place],
            final_send.at[i],
            final_recv.at[i],
            to_dom,
            to_repl,
        )

    for i in range(len(mates)):
        final_copy(i).start()

    def place_term(k, h):
        at = slice(h * half, (h + 1) * half)
        want = col_in[k]
        term = term_in[h, k].astype(f32)
        for c in range(blocks):
            rows = slice(c * tile, (c + 1) * tile)
            grad_features[rows, at] += term * want[c : c + 1]

    for h in range(2):
        place_term(dom, h)
        for i in range(len(steps)):
            term_copy(h, i, at_distance(*steps[i])).wait_recv()
            place_term(source(i), h)

    for i in range(len(mates)):
        final_copy(i).wait_recv()
    for p in range(shares):
        weight_grad[p * share_rows : (p + 1) * share_rows, :] = final_share[p]

    for i, (a, b) in enumerate(steps):
        peer = at_distance(a, b)
        col_copy(i, peer).wait_send()
        for h in range(2):
            feat_copy(h, i, peer).wait_send()
            term_copy(h, i, peer).wait_send()
    for h in range(2):
        part_copy(h).wait_send()
        grad_copy(h).wait_send()
    for i in range(len(mates)):
        share_copy(i).wait_send()
        final_copy(i).wait_send()
    for a in range(1, planes):
        plane_copy(a).wait_send()


def fused_on_device(
    features,
    weight,
    bias_vector,
    cotangent,
    near_tiles,
    near_offsets,
    near_cols,
    far_tiles,
    far_rows,
    far_cols,
):
    rows_dev, feat = features.shape
    tile = near_tiles.shape[1]
    near_count = near_tiles.shape[0]
    dom_count = lax.axis_size("dom")
    half = feat // 2
    peers = dom_count - 1
    shares = 2 * FAST_PLANE
    mates = shares - 1
    planes = dom_count // FAST_PLANE
    blocks = rows_dev // tile
    near_rows = slot_rows(near_offsets[0], near_count)
    hot = (
        membership_flags(near_rows, 2 * blocks, jnp.float32),
        membership_flags(near_cols[0], blocks, jnp.float32),
        membership_flags(far_rows.reshape(-1), 2 * blocks, jnp.float32),
        membership_flags(far_cols.reshape(-1), blocks, jnp.float32),
    )
    flags = jnp.concatenate([part.reshape(-1) for part in hot])
    scale = 1.0 / math.sqrt(rows_dev * dom_count * 2)
    bf16, f32 = jnp.bfloat16, jnp.float32
    vmem = pl.BlockSpec(memory_space=pltpu.VMEM)
    hbm = pl.BlockSpec(memory_space=pltpu.HBM)
    dma = pltpu.SemaphoreType.DMA
    return pl.pallas_call(
        functools.partial(layer_kernel, dom_count, near_count, scale),
        out_shape=(
            jax.ShapeDtypeStruct((rows_dev, feat), bf16),
            jax.ShapeDtypeStruct((rows_dev, feat), f32),
            jax.ShapeDtypeStruct((feat, feat), f32),
        ),
        in_specs=[pl.BlockSpec(memory_space=pltpu.SMEM)] + [hbm, hbm, vmem, hbm, hbm, hbm],
        out_specs=(vmem, vmem, vmem),
        scratch_shapes=[
            pltpu.VMEM((rows_dev, feat), f32),
            pltpu.VMEM((feat, feat), bf16),
            pltpu.VMEM((rows_dev, feat), bf16),
            pltpu.VMEM((near_count, tile, tile), bf16),
            pltpu.VMEM((dom_count, tile, tile), bf16),
            dma((5,)),
            pltpu.VMEM((2, rows_dev, half), bf16),
            pltpu.VMEM((dom_count, 8, half), f32),
            pltpu.VMEM((dom_count, 8, half), f32),
            pltpu.VMEM((2, peers, tile, half), bf16),
            pltpu.VMEM((2, dom_count * tile, half), bf16),
            pltpu.VMEM((2 * rows_dev, rows_dev + dom_count * tile), bf16),
            pltpu.VMEM((dom_count, tile, tile), bf16),
            pltpu.VMEM((near_count, tile, tile), bf16),
            pltpu.VMEM((2, rows_dev, half), bf16),
            pltpu.VMEM((2, rows_dev, half), bf16),
            pltpu.VMEM((2, rows_dev, half), f32),
            pltpu.VMEM((rows_dev, feat), bf16),
            pltpu.VMEM((rows_dev, feat), bf16),
            pltpu.VMEM((2, 2 * rows_dev, half), bf16),
            pltpu.VMEM((2, peers, tile, half), bf16),
            pltpu.VMEM((2, dom_count, tile, half), bf16),
            pltpu.VMEM((shares, feat // shares, feat), bf16),
            pltpu.VMEM((shares, feat // shares, feat), bf16),
            pltpu.VMEM((planes, feat // shares, feat), bf16),
            pltpu.VMEM((shares, feat // shares, feat), f32),
            dma((peers,)),
            dma((peers,)),
            dma((2, peers)),
            dma((2, peers)),
            dma((2,)),
            dma((2,)),
            dma((2,)),
            dma((2,)),
            dma((2, peers)),
            dma((2, peers)),
            dma((mates,)),
            dma((mates,)),
            dma((planes - 1,)),
            dma((planes - 1,)),
            dma((mates,)),
            dma((mates,)),
        ],
        compiler_params=pltpu.CompilerParams(
            collective_id=0, has_side_effects=True, vmem_limit_bytes=60 * 1024 * 1024
        ),
    )(
        flags,
        features,
        weight,
        bias_vector.reshape(1, feat),
        cotangent,
        near_tiles,
        far_tiles.reshape(dom_count, tile, tile),
    )


def fits_one_kernel(mesh):
    return mesh.shape["repl"] == 2 and mesh.shape["dom"] == 4 * FAST_PLANE


def solution(mesh):
    placed = (
        P(("dom", "repl"), None),
        P(),
        P(),
        P(("dom", "repl"), None),
        P(("dom", "repl"), None, None),
        P(("dom", "repl"), None),
        P(("dom", "repl"), None),
        P(("dom", "repl"), None, None, None, None),
        P(("dom", "repl"), None, None),
        P(("dom", "repl"), None, None),
    )
    return jax.shard_map(
        fused_on_device if fits_one_kernel(mesh) else on_device,
        mesh=mesh,
        in_specs=placed,
        out_specs=(P(("dom", "repl"), None), P(("dom", "repl"), None), P()),
        check_vma=False,
    )
```
